32 devices in a mesh: label: 16 (over z, y, x), query: 2 (over core).
Axes of the slice: x: 2, y: 2, z: 4, core: 2. Of those that a mesh axis runs over, the one named last changes fastest.
Arguments:
- queries: bfloat16 [384, 768], P('query'), may hold values from -6 to 6
- label_ids: int32 [384, 10], P('query'), may hold values from 0 to 1023, as said below
- label_text: bfloat16 [1024, 32, 768], P('label'), may hold values from -6 to 6
- up_weight: bfloat16 [768, 3072], P(None, 'query'), may hold values from -0.21875 to 0.21875
- down_weight: bfloat16 [768, 3072], P(None, 'query'), may hold values from -0.109375 to 0.109375
- free_vectors: float32 [1024, 768], P('label'), may hold values from -4 to 4
- moments: float32 [1024, 768], P('label'), may hold values from -0.06 to 0.06
- seconds: float32 [1024, 768], P('label'), may hold values from 1e-05 to 0.001
Outputs:
- free_new: float32 [1024, 768], P('label')
- moments_new: float32 [1024, 768], P('label')
- seconds_new: float32 [1024, 768], P('label')
- query_grad: float32 [384, 768], P('query')
- up_grad: float32 [768, 3072], P('label', 'query')
- down_grad: float32 [768, 3072], P('label', 'query')
The draws below stay inside these ranges and needn't reach their ends.
Inputs may be any that keep to these rules, and one draw needn't show every extreme that they name: `label_ids`: the 10 ids of one query are distinct.
All inputs are finite; a program needn't handle non-finite values.
Results may differ from the reference program's by a relative error of at most 0.023.
Values sent between devices are 32-bit elements; how exact they have to be, the bound alone decides.
No kernel may reach another device: no remote copies, remote signals or barrier semaphores. Data moves between devices by JAX's collectives and lax.ppermute only.
A program may use at most 64 MiB of HBM per device.

```python
import math
import jax
import jax.numpy as jnp
from jax import lax

D = 768
FF = 3072
K = 10
TEXT_LEN = 32
LAB_DEV = 64
LABELS = 1024
QUERIES = 384


def draw_label_ids(key, part):
    rate_key = jax.random.fold_in(key, 11)
    pick_key = jax.random.fold_in(key, 12)
    jitter_key = jax.random.fold_in(key, 13)
    shard_count = LABELS // LAB_DEV
    column = jnp.arange(LABELS, dtype=jnp.int32)
    exponent = jax.random.randint(rate_key, (shard_count,), 0, 4)
    shard_rates = jnp.left_shift(jnp.ones((shard_count,), jnp.int32), exponent)
    label_rates = shard_rates[column // LAB_DEV]
    picked = jax.random.randint(pick_key, (LABELS,), 0, 16)
    end_labels = jnp.logical_or(column == 0, column == LABELS - 1)
    eligible = jnp.logical_or(picked < label_rates, end_labels).astype(jnp.int32)
    first_row = (jnp.arange(QUERIES, dtype=jnp.int32) == 0)[:, None]
    levels = eligible[None, :] + 2 * jnp.logical_and(first_row, end_labels[None, :]).astype(jnp.int32)
    spread = max(2, 2 ** 28 // LABELS)
    jitter = jax.random.randint(jitter_key, (QUERIES, LABELS), 0, spread)
    ranked = (levels * spread + jitter) * LABELS + column[None, :]
    chosen = lax.top_k(ranked, K)[1]
    return chosen.astype(jnp.int32)


def with_spikes(entries, rng, source, target, shards_of, factor):
    owner, partner = [(jnp.arange(entries.shape[dim]) // (entries.shape[dim] // shards_of)).reshape([-1 if axis == dim else 1 for axis in range(entries.ndim)]) for dim in (source, target)]
    chosen = jax.random.permutation(rng, shards_of)[partner]
    strong = (owner == chosen) | (owner == (partner + shards_of // 2) % shards_of)
    return jnp.where(strong, factor * entries, entries)


def level_of(rng, extent, cuts, least, largest):
    def one(position, parts):
        steps = jax.random.uniform(jax.random.fold_in(jax.random.fold_in(rng, 6), position), (parts,), jnp.float32, least / len(cuts), largest / len(cuts))
        return jnp.repeat(jnp.exp(steps), extent[position] // parts).reshape((-1,) + (1,) * (len(extent) - position - 1))

    loudness = one(*cuts[0])
    for cut in cuts[1:]:
        loudness = loudness * one(*cut)
    return loudness


def noise(stream_key, dims, deviation, bound, shards=(), kind=jnp.bfloat16):
    values = jax.random.normal(stream_key, dims, jnp.float32) * deviation
    if len(shards) > 0:
        values = level_of(stream_key, dims, shards, -0.22, 0.18) * values
    return jnp.clip(values, min=-bound, max=bound).astype(kind)


def bell_draw_with(key, shape, width, reach, cuts, heavy, kind=jnp.bfloat16):
    values = width * jax.random.normal(key, shape, jnp.float32)
    if cuts:
        values = values * level_of(key, shape, cuts, -0.22, 0.18)
    return jnp.clip(with_spikes(values, jax.random.fold_in(key, 3), *heavy), -reach, reach).astype(kind)


def setup_inputs(seed: int = 0) -> dict:
    streams_of = jax.random.split(jax.random.key(seed), 9)
    queries = noise(streams_of[0], (QUERIES, D), 1.0, 6.0, ((0, 2),))
    label_ids = draw_label_ids(jax.random.fold_in(streams_of[8], 71), 0)
    label_text = bell_draw_with(streams_of[2], (LABELS, TEXT_LEN, D), 1.0, 6.0, ((0, 16),), (0, 2, 16, 2.0))
    up_weight = noise(streams_of[3], (D, FF), D ** -0.5, 0.21875, ((1, 2),))
    down_weight = noise(streams_of[4], (D, FF), FF ** -0.5, 0.109375, ((1, 2),))
    free_vectors = noise(streams_of[5], (LABELS, D), 0.5, 4.0, ((0, 16),), jnp.float32)
    moments = noise(streams_of[6], (LABELS, D), 0.01, 0.06, ((0, 16),), jnp.float32)
    seconds = jnp.clip(jnp.exp(math.log(0.001) - 4.6051703 * jax.random.uniform(streams_of[7], (LABELS, D), jnp.float32) ** level_of(streams_of[7], (LABELS, D), ((0, 16),), -0.2, 0.2)), 9.999999747378752e-06, 0.001)
    return dict(queries=queries, label_ids=label_ids, label_text=label_text, up_weight=up_weight, down_weight=down_weight, free_vectors=free_vectors, moments=moments, seconds=seconds)


beta_one = 0.9
beta_two = 0.999
adam_eps = 1e-08
learn_rate = 0.05
first_fix = 1.0 - 0.9 ** 10
second_fix = 1.0 - 0.999 ** 10

def gelu_tanh(values):
    return jax.nn.gelu(values, approximate=True)

def reference(queries, label_ids, label_text, up_weight, down_weight, free_vectors, moments, seconds):
    temper = 1.0 / jnp.sqrt(jnp.float32(D))
    block_count = LABELS // LAB_DEV
    text_blocks = label_text.reshape(block_count, LAB_DEV, TEXT_LEN, D)

    def pool_block(text_block):
        text_rows = text_block.reshape(LAB_DEV * TEXT_LEN, D)
        preact = jnp.dot(text_rows, up_weight, preferred_element_type=jnp.float32)
        hidden = gelu_tanh(preact).astype(jnp.bfloat16)
        pooled_hidden = lax.optimization_barrier(jnp.mean(hidden.reshape(LAB_DEV, TEXT_LEN, FF), axis=1, dtype=jnp.float32))
        pooled_text = lax.optimization_barrier(jnp.mean(text_block, axis=1, dtype=jnp.float32))
        return (pooled_text, pooled_hidden)
    pooled_text, pooled_hidden = lax.map(pool_block, text_blocks)
    pooled_text = pooled_text.reshape(LABELS, D)
    pooled_hidden = pooled_hidden.reshape(LABELS, FF)
    down_float = down_weight.astype(jnp.float32)
    encoded = jnp.dot(pooled_hidden, down_float.T, precision=lax.Precision.HIGHEST)
    label_vec = pooled_text + encoded + free_vectors
    label_bf = label_vec.astype(jnp.bfloat16)
    picked = label_bf[label_ids].astype(jnp.float32)
    query_f = queries.astype(jnp.float32)
    scores = jnp.einsum('id,ikd->ik', query_f, picked) * temper
    likely = jax.nn.softmax(scores, axis=-1)
    target = jnp.where(jnp.arange(K) < 2, 0.5, 0.0).astype(jnp.float32)
    pair_coef = ((likely - target[None, :]) * temper).astype(jnp.bfloat16)
    coef_f = pair_coef.astype(jnp.float32)
    query_grad = jnp.einsum('ik,ikd->id', coef_f, picked)
    terms = (coef_f[:, :, None] * query_f[:, None, :]).reshape(-1, D)
    flat_ids = label_ids.reshape(-1).astype(jnp.int32)
    label_grad = jax.ops.segment_sum(terms, flat_ids, num_segments=LABELS)
    counts = jax.ops.segment_sum(jnp.ones(flat_ids.shape, jnp.float32), flat_ids, num_segments=LABELS)
    out_grad = label_grad.astype(jnp.bfloat16)
    down_grad = jnp.dot(out_grad.astype(jnp.float32).T, pooled_hidden, precision=lax.Precision.HIGHEST)
    hidden_grad = jnp.dot(out_grad, down_weight, preferred_element_type=jnp.float32) / TEXT_LEN
    grad_blocks = hidden_grad.reshape(block_count, LAB_DEV, FF)

    def add_block(running, pieces):
        text_block, grad_block = pieces
        text_rows = text_block.reshape(LAB_DEV * TEXT_LEN, D)
        preact = jnp.dot(text_rows, up_weight, preferred_element_type=jnp.float32)
        token_grad = jnp.broadcast_to(grad_block[:, None, :], (LAB_DEV, TEXT_LEN, FF)).reshape(LAB_DEV * TEXT_LEN, FF)
        preact_grad = jax.vjp(gelu_tanh, preact)[1](token_grad)[0].astype(jnp.bfloat16)
        return (running + jnp.dot(text_rows.T, preact_grad, preferred_element_type=jnp.float32), None)
    scanned = lax.scan(add_block, jnp.zeros((D, FF), jnp.float32), (text_blocks, grad_blocks))
    up_grad = scanned[0]
    touched = (counts > 0.5)[:, None]
    moment_step = beta_one * moments + (1.0 - beta_one) * label_grad
    second_step = beta_two * seconds + (1.0 - beta_two) * label_grad * label_grad
    update = learn_rate * (moment_step / first_fix) / (jnp.sqrt(second_step / second_fix) + adam_eps)
    free_new = jnp.where(touched, free_vectors - update, free_vectors)
    moments_new = jnp.where(touched, moment_step, moments)
    seconds_new = jnp.where(touched, second_step, seconds)
    return (free_new, moments_new, seconds_new, query_grad, up_grad, down_grad)
```

```python
import functools

import jax
import jax.numpy as jnp
from jax import lax
from jax.experimental import pallas as pl
from jax.sharding import PartitionSpec as P

beta_one = 0.9
beta_two = 0.999
adam_eps = 1e-08
learn_rate = 0.05
first_fix = 1.0 - 0.9**10
second_fix = 1.0 - 0.999**10

PLANE = 4
CHUNKS = 3


def gelu_tanh(values):
    return jax.nn.gelu(values, approximate=True)


def pair_swap(values, axis, count, bits):
    return lax.ppermute(values, axis, [(s, s ^ bits) for s in range(count)])


def query_gather(values, query_count):
    if query_count != 2:
        return lax.all_gather(values, "query")
    other = pair_swap(values, "query", 2, 1)
    first = lax.axis_index("query") == 0
    return jnp.stack((jnp.where(first, values, other), jnp.where(first, other, values)))


def query_sum(values, query_count):
    if query_count != 2:
        return lax.psum(values, "query")
    return values + pair_swap(values, "query", 2, 1)


def label_sum(values, label_count):
    values = values + sum(pair_swap(values, "label", label_count, b) for b in range(1, PLANE))
    return values + sum(
        pair_swap(values, "label", label_count, b) for b in range(PLANE, label_count, PLANE)
    )


def rounded(values):
    def kernel(wide_ref, narrow_ref):
        narrow_ref[...] = wide_ref[...].astype(jnp.bfloat16)

    return pl.pallas_call(
        kernel, out_shape=jax.ShapeDtypeStruct(values.shape, jnp.bfloat16)
    )(values)


def split_bf16(values):
    high = values.astype(jnp.bfloat16)
    low = (values - high.astype(jnp.float32)).astype(jnp.bfloat16)
    return high, low


def half_exchange(blocks, axis, bit, label_count):
    mine = (lax.axis_index("label") // bit) % 2
    keep = lax.dynamic_index_in_dim(blocks, mine, axis, keepdims=False)
    give = lax.dynamic_index_in_dim(blocks, 1 - mine, axis, keepdims=False)
    return keep + pair_swap(give, "label", label_count, bit)


def scatter_sum(partial, label_count):
    rows, cols = partial.shape
    planes = label_count // PLANE
    own = rows // label_count
    half = cols // 2
    blocks = partial.reshape(planes, 2, 2, own, cols)
    left = half_exchange(blocks[..., :half], 2, 1, label_count)
    right = half_exchange(blocks[..., half:], 1, 2, label_count)
    left = half_exchange(left, 1, 2, label_count)
    right = half_exchange(right, 1, 1, label_count)
    joined = jnp.concatenate((left, right), axis=-1)
    plane = lax.axis_index("label") // PLANE
    total = lax.dynamic_index_in_dim(joined, plane, 0, keepdims=False)
    for other in range(1, planes):
        give = lax.dynamic_index_in_dim(joined, plane ^ other, 0, keepdims=False)
        total = total + pair_swap(give, "label", label_count, other * PLANE)
    return total


def gather_labels(values, label_count):
    planes = label_count // PLANE
    rows, cols = values.shape
    whole = jnp.stack(
        [values] + [pair_swap(values, "label", label_count, b * PLANE) for b in range(1, planes)]
    )
    half = cols // 2
    left, right = whole[..., :half], whole[..., half:]
    left = jnp.stack((left, pair_swap(left, "label", label_count, 2)), axis=1)
    right = jnp.stack((right, pair_swap(right, "label", label_count, 1)), axis=1)
    left = jnp.stack((left, pair_swap(left, "label", label_count, 1)), axis=2)
    right = jnp.stack((right, pair_swap(right, "label", label_count, 2)), axis=1)
    return jnp.concatenate((left, right), axis=-1).reshape(label_count, rows, cols)


def body(
    label_count,
    query_count,
    queries,
    label_ids,
    label_text,
    up_weight,
    down_weight,
    free_vectors,
    moments,
    seconds,
):
    label_rows, text_len, model_width = label_text.shape
    query_rows = queries.shape[0]
    unit_cols = up_weight.shape[1]
    labels = label_count * label_rows
    temper = 1.0 / jnp.sqrt(jnp.float32(model_width))
    shard = lax.axis_index("label")
    core = lax.axis_index("query")

    every_query = query_gather(queries.astype(jnp.float32), query_count)
    every_query = rounded(every_query.reshape(query_count * query_rows, model_width))
    ids = query_gather(label_ids.T, query_count)
    ids = jnp.moveaxis(ids, 0, 1).reshape(ids.shape[1], query_count * query_rows)

    text_rows = label_text.reshape(label_rows * text_len, model_width)
    preact = jnp.dot(text_rows, up_weight, preferred_element_type=jnp.float32)
    hidden = gelu_tanh(preact).astype(jnp.bfloat16)
    pooled_hidden = jnp.mean(
        hidden.reshape(label_rows, text_len, unit_cols), axis=1, dtype=jnp.float32
    )
    pooled_text = jnp.mean(label_text, axis=1, dtype=jnp.float32)
    pooled_high, pooled_low = split_bf16(pooled_hidden)
    encoded_two = lax.dot_general(
        jnp.concatenate((pooled_high, pooled_low)),
        down_weight,
        (((1,), (1,)), ((), ())),
        preferred_element_type=jnp.float32,
    )
    encoded = query_sum(encoded_two[:label_rows] + encoded_two[label_rows:], query_count)
    label_vec = pooled_text + encoded + free_vectors
    label_bf = label_vec.astype(jnp.bfloat16)

    local = ids - shard * label_rows
    owned = local[:, None, :] == jnp.arange(label_rows, dtype=jnp.int32)[None, :, None]
    similar = lax.dot_general(
        label_bf, every_query, (((1,), (1,)), ((), ())), preferred_element_type=jnp.float32
    )
    partial = jnp.sum(jnp.where(owned, similar[None], 0.0), axis=1)
    scores = label_sum(partial, label_count) * temper
    likely = jax.nn.softmax(scores, axis=0)
    target = jnp.where(jnp.arange(scores.shape[0]) < 2, 0.5, 0.0).astype(jnp.float32)
    pair_coef = ((likely - target[:, None]) * temper).astype(jnp.bfloat16)
    coef = pair_coef.astype(jnp.float32)

    spread = jnp.sum(jnp.where(owned, coef[:, None, :], 0.0), axis=0).astype(jnp.bfloat16)
    touched = jnp.any(owned, axis=(0, 2))[:, None]
    label_grad = jnp.dot(spread, every_query, preferred_element_type=jnp.float32)
    out_grad = label_grad.astype(jnp.bfloat16)
    hidden_grad = jnp.dot(out_grad, down_weight, preferred_element_type=jnp.float32) / text_len

    up_parts = []
    chunk = unit_cols // CHUNKS
    for part in range(CHUNKS):
        cols = slice(part * chunk, (part + 1) * chunk)
        preact = jnp.dot(text_rows, up_weight[:, cols], preferred_element_type=jnp.float32)
        token_grad = jnp.broadcast_to(
            hidden_grad[:, None, cols], (label_rows, text_len, chunk)
        ).reshape(label_rows * text_len, chunk)
        preact_grad = jax.vjp(gelu_tanh, preact)[1](token_grad)[0].astype(jnp.bfloat16)
        up_part = lax.dot_general(
            text_rows, preact_grad, (((0,), (0,)), ((), ())), preferred_element_type=jnp.float32
        )
        up_parts.append(scatter_sum(up_part, label_count))
    up_grad = jnp.concatenate(up_parts, axis=1)

    share = label_rows // query_count
    own_share = lax.dynamic_slice_in_dim(label_bf.astype(jnp.float32), core * share, share)
    gathered = gather_labels(own_share, label_count).reshape(label_count * share, model_width)
    position = ids // label_rows ^ shard
    within = ids % label_rows - core * share
    place = jnp.where((within >= 0) & (within < share), position * share + within, -1)
    spread_share = jnp.sum(
        jnp.where(
            place[:, None, :] == jnp.arange(label_count * share, dtype=jnp.int32)[None, :, None],
            coef[:, None, :],
            0.0,
        ),
        axis=0,
    ).astype(jnp.bfloat16)
    query_terms = lax.dot_general(
        spread_share,
        rounded(gathered),
        (((0,), (0,)), ((), ())),
        preferred_element_type=jnp.float32,
    ).reshape(query_count, query_rows, model_width)
    if query_count == 2:
        query_grad = lax.dynamic_index_in_dim(query_terms, core, keepdims=False) + pair_swap(
            lax.dynamic_index_in_dim(query_terms, 1 - core, keepdims=False), "query", 2, 1
        )
    else:
        query_grad = lax.dynamic_index_in_dim(
            lax.psum(query_terms, "query"), core, keepdims=False
        )

    unit_share = unit_cols // label_count
    pooled_all = lax.all_to_all(
        pooled_hidden.reshape(label_rows, label_count, unit_share).swapaxes(0, 1), "label", 0, 0
    ).reshape(labels, unit_share)
    spread_all = jnp.sum(
        jnp.where(
            ids[:, None, :] == jnp.arange(labels, dtype=jnp.int32)[None, :, None],
            coef[:, None, :],
            0.0,
        ),
        axis=0,
    ).astype(jnp.bfloat16)
    out_grad_all = jnp.dot(spread_all, every_query, preferred_element_type=jnp.float32).astype(
        jnp.bfloat16
    )
    all_high, all_low = split_bf16(pooled_all)
    down_two = lax.dot_general(
        out_grad_all,
        jnp.concatenate((all_high, all_low), axis=1),
        (((0,), (0,)), ((), ())),
        preferred_element_type=jnp.float32,
    )
    down_cols = down_two[:, :unit_share] + down_two[:, unit_share:]
    down_grad = lax.all_to_all(
        down_cols.reshape(label_count, model_width // label_count, unit_share), "label", 0, 0
    )
    down_grad = down_grad.swapaxes(0, 1).reshape(model_width // label_count, unit_cols)

    moment_step = beta_one * moments + (1.0 - beta_one) * label_grad
    second_step = beta_two * seconds + (1.0 - beta_two) * label_grad * label_grad
    update = (
        learn_rate * (moment_step / first_fix) / (jnp.sqrt(second_step / second_fix) + adam_eps)
    )
    free_new = jnp.where(touched, free_vectors - update, free_vectors)
    moments_new = jnp.where(touched, moment_step, moments)
    seconds_new = jnp.where(touched, second_step, seconds)
    return (free_new, moments_new, seconds_new, query_grad, up_grad, down_grad)


def solution(mesh):
    placed = (
        P("query", None),
        P("query", None),
        P("label", None, None),
        P(None, "query"),
        P(None, "query"),
        P("label", None),
        P("label", None),
        P("label", None),
    )
    return jax.shard_map(
        functools.partial(body, mesh.shape["label"], mesh.shape["query"]),
        mesh=mesh,
        in_specs=placed,
        out_specs=(
            P("label", None),
            P("label", None),
            P("label", None),
            P("query", None),
            P("label", "query"),
            P("label", "query"),
        ),
        check_vma=False,
    )
```

```python
import functools
import math

import jax
import jax.numpy as jnp
from jax import lax
from jax.experimental import pallas as pl
from jax.experimental.pallas import tpu as pltpu
from jax.sharding import PartitionSpec as P

beta_one = 0.9
beta_two = 0.999
adam_eps = 1e-08
learn_rate = 0.05
first_fix = 1.0 - 0.9**10
second_fix = 1.0 - 0.999**10

PLANE = 4
THIRDS = 3
GELU_ONE = math.sqrt(2.0 / math.pi)
GELU_THREE = GELU_ONE * 0.044715
MIB = 2**20


def whole(shape):
    return pl.BlockSpec(shape, lambda *_: (0,) * len(shape))


def scalar_spec():
    return pl.BlockSpec(memory_space=pltpu.SMEM)


def params(mib):
    return pltpu.CompilerParams(vmem_limit_bytes=mib * MIB)


def f32(shape):
    return jax.ShapeDtypeStruct(shape, jnp.float32)


def bf16(shape):
    return jax.ShapeDtypeStruct(shape, jnp.bfloat16)


def pair_swap(values, axis, count, bits):
    return lax.ppermute(values, axis, [(s, s ^ bits) for s in range(count)])


def label_sum_parts(values, label_count):
    values = values + sum(pair_swap(values, "label", label_count, b) for b in range(1, PLANE))
    return [values] + [
        pair_swap(values, "label", label_count, b) for b in range(PLANE, label_count, PLANE)
    ]


def bit_order(label_count, part):
    bits = [1 << b for b in range(label_count.bit_length() - 1)]
    lead = ([1, 2, 4], [2, 1, 4], [4, 1, 2])[part]
    return [b for b in lead if b in bits] + [b for b in bits if b not in lead]


def relative_shards(label_count, order):
    count = len(order)
    return [
        sum(bit for place, bit in enumerate(order) if p >> (count - 1 - place) & 1)
        for p in range(label_count)
    ]


def scatter_sum(keep, give, label_count, order):
    parts = [keep]
    for bit in order:
        parts.append(pair_swap(give, "label", label_count, bit))
        size = parts[-1].shape[0]
        if size == 1:
            break
        give = sum(p[size // 2 : size] for p in parts)
    return sum(p[0] for p in parts)


def split_bf16(values):
    high = values.astype(jnp.bfloat16)
    low = (values - high.astype(jnp.float32)).astype(jnp.bfloat16)
    return high, low


def encode(text_rows, up_weight, down_weight, label_rows):
    tokens, model_width = text_rows.shape
    unit_cols = up_weight.shape[1]
    text_len = tokens // label_rows
    steps = 8
    rows = tokens // steps
    pools = label_rows // steps
    chunk = unit_cols // THIRDS

    def kernel(text_ref, up_ref, down_ref, pooled_ref, slope_ref, turned_ref, encoded_ref):
        step = pl.program_id(0)
        text = text_ref[...]
        turned_ref[...] = text.T
        for part in range(THIRDS):
            cols = slice(part * chunk, (part + 1) * chunk)
            x = jnp.dot(text, up_ref[:, cols], preferred_element_type=jnp.float32)
            square = x * x
            gate = 0.5 + 0.5 * jnp.tanh(x * (GELU_ONE + GELU_THREE * square))
            hidden = x * gate
            slope = gate + (hidden - hidden * gate) * (2 * GELU_ONE + 6 * GELU_THREE * square)
            slope_ref[:, cols] = slope.astype(jnp.bfloat16)
            pooled_ref[pl.ds(step * pools, pools), cols] = jnp.sum(
                hidden.reshape(pools, text_len, chunk), axis=1
            ) * (1.0 / text_len)

        @pl.when(step == steps - 1)
        def _():
            high, low = split_bf16(pooled_ref[...])
            both = lax.dot_general(
                jnp.concatenate((high, low)),
                down_ref[...],
                (((1,), (1,)), ((), ())),
                preferred_element_type=jnp.float32,
            )
            encoded_ref[...] = both[:label_rows] + both[label_rows:]

    return pl.pallas_call(
        kernel,
        grid=(steps,),
        in_specs=[
            pl.BlockSpec((rows, model_width), lambda i: (i, 0)),
            whole(up_weight.shape),
            whole(down_weight.shape),
        ],
        out_specs=[
            whole((label_rows, unit_cols)),
            pl.BlockSpec((rows, unit_cols), lambda i: (i, 0)),
            pl.BlockSpec((model_width, rows), lambda i: (0, i)),
            whole((label_rows, model_width)),
        ],
        out_shape=[
            f32((label_rows, unit_cols)),
            bf16((tokens, unit_cols)),
            bf16((model_width, tokens)),
            f32((label_rows, model_width)),
        ],
        compiler_params=params(28),
        name="encode",
    )(text_rows, up_weight, down_weight)


def score(place, encoded, pooled_text, free_vectors, query_pieces, ids, share):
    label_rows, model_width = free_vectors.shape
    choices, total = ids.shape
    terms = len(encoded)
    pieces = len(query_pieces)

    def kernel(place_ref, *refs):
        encoded_refs, refs = refs[:terms], refs[terms:]
        pooled_ref, free_ref, *refs = refs
        query_refs, refs = refs[:pieces], refs[pieces:]
        ids_ref, share_ref, every_ref, partial_ref, label_ref = refs
        label_vec = pooled_ref[...] + sum(r[...] for r in encoded_refs) + free_ref[...]
        label_bf = label_vec.astype(jnp.bfloat16)
        label_ref[...] = label_bf.astype(jnp.float32)
        share_ref[...] = label_ref[pl.ds(pl.multiple_of(place_ref[1], share), share), :]
        row = 0
        for ref in query_refs:
            every_ref[row : row + ref.shape[0], :] = ref[...].astype(jnp.bfloat16)
            row += ref.shape[0]
        similar = lax.dot_general(
            label_bf, every_ref[...], (((1,), (1,)), ((), ())), preferred_element_type=jnp.float32
        )
        label = lax.broadcasted_iota(jnp.int32, (label_rows, total), 0) + place_ref[0]
        for k in range(choices):
            partial_ref[k : k + 1, :] = jnp.sum(
                jnp.where(label == ids_ref[k : k + 1, :], similar, 0.0), axis=0, keepdims=True
            )

    return pl.pallas_call(
        kernel,
        in_specs=[scalar_spec()] + [pl.BlockSpec(memory_space=pltpu.VMEM)] * (terms + pieces + 3),
        out_shape=[
            f32((share, model_width)),
            bf16((total, model_width)),
            f32((choices, total)),
        ],
        scratch_shapes=[pltpu.VMEM((label_rows, model_width), jnp.float32)],
        compiler_params=params(24),
        name="score",
    )(place, *encoded, pooled_text, free_vectors, *query_pieces, ids)


def spread_of(ids_ref, coef, first, labels):
    choices, total = coef.shape
    label = lax.broadcasted_iota(jnp.int32, (labels, total), 0) + first
    spread = jnp.zeros((labels, total), jnp.float32)
    for k in range(choices):
        spread = jnp.where(label == ids_ref[k : k + 1, :total], coef[k : k + 1, :], spread)
    return spread.astype(jnp.bfloat16)


def label_gradient(place, score_terms, ids, every_query, down_weight, label_rows, text_len):
    choices, total = ids.shape
    model_width, unit_cols = down_weight.shape
    terms = len(score_terms)
    temper = 1.0 / math.sqrt(model_width)

    def kernel(place_ref, *refs):
        score_refs, refs = refs[:terms], refs[terms:]
        ids_ref, query_ref, down_ref, coef_ref, grad_ref, hidden_ref = refs
        scores = sum(r[...] for r in score_refs) * temper
        powers = jnp.exp(scores - jnp.max(scores, axis=0, keepdims=True))
        likely = powers / jnp.sum(powers, axis=0, keepdims=True)
        rank = lax.broadcasted_iota(jnp.int32, (choices, total), 0)
        coef = (likely - jnp.where(rank < 2, 0.5, 0.0)) * temper
        coef = coef.astype(jnp.bfloat16).astype(jnp.float32)
        coef_ref[...] = coef
        spread = spread_of(ids_ref, coef, place_ref[0], label_rows)
        grad = jnp.dot(spread, query_ref[...], preferred_element_type=jnp.float32)
        grad_ref[...] = grad
        hidden_ref[...] = jnp.dot(
            grad.astype(jnp.bfloat16), down_ref[...], preferred_element_type=jnp.float32
        ) * (1.0 / text_len)

    return pl.pallas_call(
        kernel,
        in_specs=[scalar_spec()] + [pl.BlockSpec(memory_space=pltpu.VMEM)] * (terms + 3),
        out_shape=[f32((choices, total)), f32((label_rows, model_width)), f32((label_rows, unit_cols))],
        compiler_params=params(24),
        name="label_gradient",
    )(place, *score_terms, ids, every_query, down_weight)


def up_gradient(place, turned, slope, hidden_grad, label_count, part):
    model_width, tokens = turned.shape
    label_rows, unit_cols = hidden_grad.shape
    text_len = tokens // label_rows
    cols = unit_cols // THIRDS
    own = model_width // label_count
    steps = 4
    depth = tokens // steps
    rows = label_rows // steps
    relative = relative_shards(label_count, bit_order(label_count, part))
    half = label_count // 2

    def kernel(place_ref, turned_ref, slope_ref, hidden_ref, keep_ref, give_ref, total_ref, blocks_ref):
        step = pl.program_id(0)
        slope = slope_ref[...].astype(jnp.float32).reshape(rows, text_len, cols)
        grad = slope * hidden_ref[...][:, None, :]
        grad = grad.reshape(depth, cols).astype(jnp.bfloat16)
        term = jnp.dot(turned_ref[...], grad, preferred_element_type=jnp.float32)

        @pl.when(step == 0)
        def _():
            total_ref[...] = term

        @pl.when(step > 0)
        def _():
            total_ref[...] += term

        @pl.when(step == steps - 1)
        def _():
            for block in range(label_count):
                blocks_ref[block] = total_ref[block * own : (block + 1) * own, :]
            for p in range(half):
                keep_ref[p] = blocks_ref[place_ref[0] ^ relative[p]]
                give_ref[p] = blocks_ref[place_ref[0] ^ relative[half + p]]

    return pl.pallas_call(
        kernel,
        grid=(steps,),
        in_specs=[
            scalar_spec(),
            pl.BlockSpec((model_width, depth), lambda i: (0, i)),
            pl.BlockSpec((depth, cols), lambda i: (i, part)),
            pl.BlockSpec((rows, cols), lambda i: (i, part)),
        ],
        out_specs=[whole((half, own, cols))] * 2,
        out_shape=[f32((half, own, cols))] * 2,
        scratch_shapes=[
            pltpu.VMEM((model_width, cols), jnp.float32),
            pltpu.VMEM((label_count, own, cols), jnp.float32),
        ],
        compiler_params=params(24),
        name="up_gradient",
    )(place, turned, slope, hidden_grad)


def query_gradient(coef, ids, label_all, first, count):
    labels, model_width = label_all.shape

    def kernel(coef_ref, ids_ref, label_ref, out_ref):
        spread = spread_of(ids_ref, coef_ref[...], 0, labels)
        out_ref[...] = lax.dot_general(
            spread,
            label_ref[...].astype(jnp.bfloat16),
            (((0,), (0,)), ((), ())),
            preferred_element_type=jnp.float32,
        )

    coef = lax.dynamic_slice_in_dim(coef, first, count, 1)
    ids = lax.dynamic_slice_in_dim(ids, first, count, 1)
    return pl.pallas_call(
        kernel,
        out_shape=f32((count, model_width)),
        compiler_params=params(32),
        name="query_gradient",
    )(coef, ids, label_all)


def down_gradient(coef, ids, every_query, pooled_all, label_count):
    labels, units = pooled_all.shape
    model_width = every_query.shape[1]
    own = model_width // label_count

    def kernel(coef_ref, ids_ref, query_ref, pooled_ref, out_ref):
        spread = spread_of(ids_ref, coef_ref[...], 0, labels)
        grad = jnp.dot(spread, query_ref[...], preferred_element_type=jnp.float32)
        grad = grad.astype(jnp.bfloat16)
        total = sum(
            lax.dot_general(grad, half, (((0,), (0,)), ((), ())), preferred_element_type=jnp.float32)
            for half in split_bf16(pooled_ref[...])
        )
        for block in range(label_count):
            out_ref[block] = total[block * own : (block + 1) * own, :]

    return pl.pallas_call(
        kernel,
        out_shape=f32((label_count, own, units)),
        compiler_params=params(32),
        name="down_gradient",
    )(coef, ids, every_query, pooled_all)


def body(
    label_count,
    query_count,
    queries,
    label_ids,
    label_text,
    up_weight,
    down_weight,
    free_vectors,
    moments,
    seconds,
):
    label_rows, text_len, model_width = label_text.shape
    query_rows = queries.shape[0]
    unit_cols = up_weight.shape[1]
    labels = label_count * label_rows
    shard = lax.axis_index("label")
    core = lax.axis_index("query")
    share = label_rows // query_count
    place = jnp.stack((shard * label_rows, core * share)).astype(jnp.int32)
    shard_place = shard.astype(jnp.int32).reshape(1)

    if query_count == 2:
        query_pieces = [queries, pair_swap(queries.astype(jnp.float32), "query", 2, 1)]
        ids = jnp.concatenate((label_ids.T, pair_swap(label_ids.T, "query", 2, 1)), axis=1)
        first_query = 0
    else:
        query_pieces = [lax.all_gather(queries.astype(jnp.float32), "query", tiled=True)]
        ids = lax.all_gather(label_ids, "query", tiled=True).T
        first_query = core * query_rows

    text_rows = label_text.reshape(label_rows * text_len, model_width)
    pooled_hidden, slope, turned, encoded_part = encode(
        text_rows, up_weight, down_weight, label_rows
    )
    pooled_text = jnp.mean(label_text, axis=1, dtype=jnp.float32)
    if query_count == 2:
        encoded = [encoded_part, pair_swap(encoded_part, "query", 2, 1)]
    else:
        encoded = [lax.psum(encoded_part, "query")]
    own_share, every_query, partial = score(
        place, encoded, pooled_text, free_vectors, query_pieces, ids, share
    )
    label_all = lax.all_gather(own_share, ("label", "query"), tiled=True)
    unit_share = unit_cols // label_count
    pooled_all = lax.all_to_all(
        pooled_hidden.reshape(label_rows, label_count, unit_share).swapaxes(0, 1), "label", 0, 0
    ).reshape(labels, unit_share)

    coef, label_grad, hidden_grad = label_gradient(
        place,
        label_sum_parts(partial, label_count),
        ids,
        every_query,
        down_weight,
        label_rows,
        text_len,
    )

    up_parts = []
    for part in range(THIRDS):
        keep, give = up_gradient(shard_place, turned, slope, hidden_grad, label_count, part)
        up_parts.append(scatter_sum(keep, give, label_count, bit_order(label_count, part)))
    up_grad = jnp.concatenate(up_parts, axis=1)

    down_cols = down_gradient(coef, ids, every_query, pooled_all, label_count)
    down_grad = lax.all_to_all(down_cols, "label", 0, 0)
    down_grad = down_grad.swapaxes(0, 1).reshape(model_width // label_count, unit_cols)

    query_grad = query_gradient(coef, ids, label_all, first_query, query_rows)

    touched = jnp.any(
        (ids - shard * label_rows)[:, None, :]
        == jnp.arange(label_rows, dtype=jnp.int32)[None, :, None],
        axis=(0, 2),
    )[:, None]
    moment_step = beta_one * moments + (1.0 - beta_one) * label_grad
    second_step = beta_two * seconds + (1.0 - beta_two) * label_grad * label_grad
    update = (
        learn_rate * (moment_step / first_fix) / (jnp.sqrt(second_step / second_fix) + adam_eps)
    )
    free_new = jnp.where(touched, free_vectors - update, free_vectors)
    moments_new = jnp.where(touched, moment_step, moments)
    seconds_new = jnp.where(touched, second_step, seconds)
    return (free_new, moments_new, seconds_new, query_grad, up_grad, down_grad)


def solution(mesh):
    placed = (
        P("query", None),
        P("query", None),
        P("label", None, None),
        P(None, "query"),
        P(None, "query"),
        P("label", None),
        P("label", None),
        P("label", None),
    )
    return jax.shard_map(
        functools.partial(body, mesh.shape["label"], mesh.shape["query"]),
        mesh=mesh,
        in_specs=placed,
        out_specs=(
            P("label", None),
            P("label", None),
            P("label", None),
            P("query", None),
            P("label", "query"),
            P("label", "query"),
        ),
        check_vma=False,
    )
```

```python
import functools
import math

import jax
import jax.numpy as jnp
from jax import lax
from jax.experimental import pallas as pl
from jax.experimental.pallas import tpu as pltpu
from jax.sharding import PartitionSpec as P

beta_one = 0.9
beta_two = 0.999
adam_eps = 1e-08
learn_rate = 0.05
first_fix = 1.0 - 0.9**10
second_fix = 1.0 - 0.999**10

PLANE = 4
THIRDS = 3
GELU_ONE = math.sqrt(2.0 / math.pi)
GELU_THREE = GELU_ONE * 0.044715
MIB = 2**20
ENCODE = 28
SCORE = 24
BACKWARD = 32
REST = 24


def whole(shape):
    return pl.BlockSpec(shape, lambda *_: (0,) * len(shape))


def params(mib):
    return pltpu.CompilerParams(vmem_limit_bytes=mib * MIB)


def f32(shape):
    return jax.ShapeDtypeStruct(shape, jnp.float32)


def bf16(shape):
    return jax.ShapeDtypeStruct(shape, jnp.bfloat16)


def pair_swap(values, axis, count, bits):
    return lax.ppermute(values, axis, [(s, s ^ bits) for s in range(count)])


def parity_swap(values, counts, bits):
    label_count, query_count = counts
    return lax.ppermute(
        values,
        ("label", "query"),
        [
            (s * query_count + q, (s ^ bits[q % 2]) * query_count + q)
            for s in range(label_count)
            for q in range(query_count)
        ],
    )


def plane_sum(values, label_count):
    return values + sum(pair_swap(values, "label", label_count, b) for b in range(1, PLANE))


def plane_terms(values, label_count):
    return [values] + [
        pair_swap(values, "label", label_count, b) for b in range(PLANE, label_count, PLANE)
    ]


def bit_orders(label_count):
    bits = [1 << b for b in range(label_count.bit_length() - 1)]
    return [lead + bits[3:] for lead in ([1, 4, 2], [2, 1, 4], [4, 2, 1])]


def relative_shards(label_count, order):
    count = len(order)
    return [
        sum(bit for place, bit in enumerate(order) if p >> (count - 1 - place) & 1)
        for p in range(label_count)
    ]


def upper(parts):
    size = parts[-1].shape[0]
    return sum(p[size // 2 : size] for p in parts)


def scatter_sum(keeps, gives, label_count, before):
    orders = bit_orders(label_count)

    def swap(values, bit):
        return pair_swap(values, "label", label_count, bit)

    thirds = [[keep, swap(give, order[0])] for keep, give, order in zip(keeps, gives, orders)]
    for step in range(1, 3):
        gives = before[step - 1]([upper(parts) for parts in thirds])
        for parts, give, order in zip(thirds, gives, orders):
            parts.append(swap(give, order[step]))
    size = thirds[0][-1].shape[0]
    parts = [jnp.concatenate([sum(p[:size] for p in third) for third in thirds], axis=2)]
    for step in range(3, len(orders[0])):
        give = upper(parts)
        if step == 3:
            (give,) = before[2]([give])
        parts.append(swap(give, orders[0][step]))
    return sum(p[0] for p in parts)


def after(values, *gates):
    return lax.optimization_barrier((values, gates))[0]


def gather_planes(values, label_count):
    return jnp.stack(
        [values]
        + [pair_swap(values, "label", label_count, b) for b in range(PLANE, label_count, PLANE)]
    )


def gather_near(whole_planes, counts):
    return jnp.stack((whole_planes, parity_swap(whole_planes, counts, (1, 2))))


def gather_far(near, counts):
    return jnp.concatenate((near, parity_swap(near, counts, (2, 1))))


def split_bf16(values):
    high = values.astype(jnp.bfloat16)
    low = (values - high.astype(jnp.float32)).astype(jnp.bfloat16)
    return high, low


def gate_of(x):
    square = x * x
    inner = x * (jnp.bfloat16(GELU_ONE) + jnp.bfloat16(GELU_THREE) * square)
    return jnp.bfloat16(0.5) + jnp.bfloat16(0.5) * jnp.tanh(inner), square


def column_steps(cols):
    return 6 if cols % (6 * 128) == 0 else 3


def encode(text_rows, up_weight, down_weight, label_rows, label_count):
    tokens, model_width = text_rows.shape
    unit_cols = up_weight.shape[1]
    text_len = tokens // label_rows
    steps = column_steps(unit_cols)
    chunk = unit_cols // steps
    width = model_width // steps
    share = unit_cols // label_count

    def pool(values):
        values = values.astype(jnp.float32).reshape(label_rows, text_len, values.shape[1])
        return jnp.sum(values, axis=1) * (1.0 / text_len)

    def kernel(
        text_ref,
        up_ref,
        down_ref,
        shares_ref,
        slope_ref,
        turned_ref,
        mean_ref,
        encoded_ref,
        pooled_ref,
    ):
        step = pl.program_id(0)
        x = jnp.dot(text_ref[...], up_ref[...], preferred_element_type=jnp.float32)
        x = x.astype(jnp.bfloat16)
        gate, square = gate_of(x)
        hidden = x * gate
        inner = jnp.bfloat16(2 * GELU_ONE) + jnp.bfloat16(6 * GELU_THREE) * square
        slope_ref[...] = gate + (hidden - hidden * gate) * inner
        pooled_ref[:, pl.ds(pl.multiple_of(step * chunk, chunk), chunk)] = pool(hidden)
        some = text_ref[:, pl.ds(pl.multiple_of(step * width, width), width)]
        turned_ref[...] = some.T
        mean_ref[...] = pool(some)

        @pl.when(step == steps - 1)
        def _():
            pooled = pooled_ref[...]
            for place in range(label_count):
                shares_ref[place] = pooled[:, place * share : (place + 1) * share]
            both = lax.dot_general(
                jnp.concatenate(split_bf16(pooled)),
                down_ref[...],
                (((1,), (1,)), ((), ())),
                preferred_element_type=jnp.float32,
            )
            encoded_ref[...] = both[:label_rows] + both[label_rows:]

    return pl.pallas_call(
        kernel,
        grid=(steps,),
        in_specs=[
            whole(text_rows.shape),
            pl.BlockSpec((model_width, chunk), lambda i: (0, i)),
            whole(down_weight.shape),
        ],
        out_specs=[
            whole((label_count, label_rows, share)),
            pl.BlockSpec((tokens, chunk), lambda i: (0, i)),
            pl.BlockSpec((width, tokens), lambda i: (i, 0)),
            pl.BlockSpec((label_rows, width), lambda i: (0, i)),
            whole((label_rows, model_width)),
        ],
        out_shape=[
            f32((label_count, label_rows, share)),
            bf16((tokens, unit_cols)),
            bf16((model_width, tokens)),
            f32((label_rows, model_width)),
            f32((label_rows, model_width)),
        ],
        scratch_shapes=[pltpu.VMEM((label_rows, unit_cols), jnp.float32)],
        compiler_params=params(ENCODE),
        name="encode",
    )(text_rows, up_weight, down_weight)


def score(encoded, pooled_text, free_vectors, query_pieces, id_pieces, share):
    label_rows, model_width = free_vectors.shape
    choices = id_pieces[0].shape[0]
    total = sum(p.shape[1] for p in id_pieces)
    terms = len(encoded)
    pieces = len(query_pieces)

    def kernel(*refs):
        encoded_refs, refs = refs[:terms], refs[terms:]
        pooled_ref, free_ref, *refs = refs
        query_refs, refs = refs[:pieces], refs[pieces:]
        id_refs, refs = refs[:pieces], refs[pieces:]
        share_ref, every_ref, ids_ref, partial_ref, label_ref = refs
        core = lax.axis_index("query")
        label_vec = pooled_ref[...] + sum(r[...] for r in encoded_refs) + free_ref[...]
        label_bf = label_vec.astype(jnp.bfloat16)
        label_ref[...] = label_bf.astype(jnp.float32)
        share_ref[...] = label_ref[pl.ds(pl.multiple_of(core * share, share), share), :]
        if pieces == 1:
            every_ref[...] = query_refs[0][...].astype(jnp.bfloat16)
            ids_ref[...] = id_refs[0][...]
        else:
            rows = total // 2
            for place, ref in enumerate(query_refs):
                first = pl.multiple_of((core ^ place) * rows, rows)
                every_ref[pl.ds(first, rows), :] = ref[...].astype(jnp.bfloat16)
            own, other = (r[...] for r in id_refs)
            own_first = core == 0
            ids_ref[...] = jnp.concatenate(
                (jnp.where(own_first, own, other), jnp.where(own_first, other, own)), axis=1
            )
        similar = lax.dot_general(
            label_bf, every_ref[...], (((1,), (1,)), ((), ())), preferred_element_type=jnp.float32
        )
        label = lax.broadcasted_iota(jnp.int32, (label_rows, total), 0)
        label = label + lax.axis_index("label") * label_rows
        for k in range(choices):
            partial_ref[k : k + 1, :] = jnp.sum(
                jnp.where(label == ids_ref[k : k + 1, :], similar, 0.0), axis=0, keepdims=True
            )

    return pl.pallas_call(
        kernel,
        out_shape=[
            f32((share, model_width)),
            bf16((total, model_width)),
            jax.ShapeDtypeStruct((choices, total), jnp.int32),
            f32((choices, total)),
        ],
        scratch_shapes=[pltpu.VMEM((label_rows, model_width), jnp.float32)],
        compiler_params=params(SCORE),
        name="score",
    )(*encoded, pooled_text, free_vectors, *query_pieces, *id_pieces)


def spread_of(ids_ref, coef, first, labels):
    choices, total = coef.shape
    label = lax.broadcasted_iota(jnp.int32, (labels, total), 0) + first
    spread = jnp.zeros((labels, total), jnp.float32)
    for k in range(choices):
        spread = jnp.where(label == ids_ref[k : k + 1, :], coef[k : k + 1, :], spread)
    return spread.astype(jnp.bfloat16)


def backward(score_terms, ids, every_query, down_weight, turned, slope, label_rows, label_count):
    choices, total = ids.shape
    model_width, unit_cols = down_weight.shape
    tokens = turned.shape[1]
    text_len = tokens // label_rows
    cols = unit_cols // THIRDS
    own = model_width // label_count
    half = label_count // 2
    terms = len(score_terms)
    temper = 1.0 / math.sqrt(model_width)
    relative = [relative_shards(label_count, order) for order in bit_orders(label_count)]

    def kernel(*refs):
        score_refs, refs = refs[:terms], refs[terms:]
        shard = lax.axis_index("label")
        ids_ref, query_ref, down_ref, *refs = refs
        turned_ref, slope_ref, coef_ref, grad_ref, *refs = refs
        outs, refs = refs[: 2 * THIRDS], refs[2 * THIRDS :]
        blocks_ref, kept_ref, given_ref, out_sem = refs

        scores = sum(r[...] for r in score_refs) * temper
        powers = jnp.exp(scores - jnp.max(scores, axis=0, keepdims=True))
        likely = powers / jnp.sum(powers, axis=0, keepdims=True)
        rank = lax.broadcasted_iota(jnp.int32, (choices, total), 0)
        coef = (likely - jnp.where(rank < 2, 0.5, 0.0)) * temper
        coef = coef.astype(jnp.bfloat16).astype(jnp.float32)
        coef_ref[...] = coef
        spread = spread_of(ids_ref, coef, shard * label_rows, label_rows)
        grad = jnp.dot(spread, query_ref[...], preferred_element_type=jnp.float32)
        grad_ref[...] = grad
        out_grad = grad.astype(jnp.bfloat16)

        flights = []
        for third in range(THIRDS):
            span = slice(third * cols, (third + 1) * cols)
            hidden_grad = jnp.dot(
                out_grad, down_ref[:, span], preferred_element_type=jnp.float32
            ) * (1.0 / text_len)
            preact_grad = (
                slope_ref[:, span].astype(jnp.float32).reshape(label_rows, text_len, cols)
                * hidden_grad[:, None, :]
            )
            up_term = jnp.dot(
                turned_ref[...],
                preact_grad.reshape(tokens, cols).astype(jnp.bfloat16),
                preferred_element_type=jnp.float32,
            )
            for block in range(label_count):
                blocks_ref[block] = up_term[block * own : (block + 1) * own, :]
            for p in range(half):
                given_ref[third, p] = blocks_ref[shard ^ relative[third][half + p]]
                kept_ref[third, p] = blocks_ref[shard ^ relative[third][p]]
            for side, buffer in enumerate((kept_ref, given_ref)):
                place = 2 * third + side
                flight = pltpu.make_async_copy(buffer.at[third], outs[place], out_sem.at[place])
                flight.start()
                flights.append(flight)
        for flight in flights:
            flight.wait()

    outs = pl.pallas_call(
        kernel,
        in_specs=[pl.BlockSpec(memory_space=pltpu.VMEM)] * (terms + 5),
        out_specs=[pl.BlockSpec(memory_space=pltpu.VMEM)] * 2
        + [pl.BlockSpec(memory_space=pl.ANY)] * (2 * THIRDS),
        out_shape=[f32((choices, total)), f32((label_rows, model_width))]
        + [f32((half, own, cols))] * (2 * THIRDS),
        scratch_shapes=[pltpu.VMEM((label_count, own, cols), jnp.float32)]
        + [pltpu.VMEM((THIRDS, half, own, cols), jnp.float32)] * 2
        + [pltpu.SemaphoreType.DMA((2 * THIRDS,))],
        compiler_params=params(BACKWARD),
        cost_estimate=pl.CostEstimate(
            flops=2 * tokens * model_width * unit_cols,
            bytes_accessed=16 * MIB,
            transcendentals=choices * total,
        ),
        name="backward",
    )(*score_terms, ids, every_query, down_weight, turned, slope)
    return outs[0], outs[1], outs[2::2], outs[3::2]


def query_gradient(coef, ids, vectors, label_rows):
    choices, total = ids.shape
    near, planes, share, model_width = vectors.shape
    rows = near * planes * share

    def kernel(coef_ref, ids_ref, vector_ref, out_ref):
        core = lax.axis_index("query")
        row = lax.broadcasted_iota(jnp.int32, (rows, total), 0)
        block = row // share
        plane, place = block % planes, block // planes
        turned = place // 2 + place % 2 * 2
        place = jnp.where(lax.rem(core, 2) == 0, place, turned)
        owner = lax.axis_index("label") ^ (plane * PLANE + place)
        label = owner * label_rows + core * share + row % share
        spread = jnp.zeros((rows, total), jnp.float32)
        for k in range(choices):
            spread = jnp.where(label == ids_ref[k : k + 1, :], coef_ref[k : k + 1, :], spread)
        out_ref[...] = lax.dot_general(
            spread.astype(jnp.bfloat16),
            vector_ref[...].reshape(rows, model_width).astype(jnp.bfloat16),
            (((0,), (0,)), ((), ())),
            preferred_element_type=jnp.float32,
        )

    return pl.pallas_call(
        kernel,
        out_shape=f32((total, model_width)),
        compiler_params=params(REST),
        name="query_gradient",
    )(coef, ids, vectors)


def down_gradient_and_adam(
    coef, ids, every_query, pooled_all, label_grad, free_vectors, moments, seconds, label_count
):
    labels, units = pooled_all.shape
    model_width = every_query.shape[1]
    label_rows = free_vectors.shape[0]
    own = model_width // label_count
    choices, total = ids.shape

    def product(left, right):
        both = lax.dot_general(
            left,
            jnp.concatenate(split_bf16(right), axis=1),
            (((0,), (0,)), ((), ())),
            preferred_element_type=jnp.float32,
        )
        return both[:, :units] + both[:, units:]

    def kernel(
        coef_ref,
        ids_ref,
        query_ref,
        pooled_ref,
        grad_ref,
        free_ref,
        moment_ref,
        second_ref,
        out_ref,
        free_out,
        moment_out,
        second_out,
    ):
        spread = spread_of(ids_ref, coef_ref[...], 0, labels)
        result = product(query_ref[...], product(spread, pooled_ref[...]))
        for block in range(label_count):
            out_ref[block] = result[block * own : (block + 1) * own, :]

        label = lax.broadcasted_iota(jnp.int32, (label_rows, total), 0)
        label = label + lax.axis_index("label") * label_rows
        hits = jnp.zeros((label_rows, total), jnp.float32)
        for k in range(choices):
            hits = jnp.where(label == ids_ref[k : k + 1, :], 1.0, hits)
        touched = jnp.max(hits, axis=1, keepdims=True) > 0.5
        grad, free, moment, second = (r[...] for r in (grad_ref, free_ref, moment_ref, second_ref))
        moment_step = beta_one * moment + (1.0 - beta_one) * grad
        second_step = beta_two * second + (1.0 - beta_two) * grad * grad
        update = (
            learn_rate
            * (moment_step / first_fix)
            / (jnp.sqrt(second_step / second_fix) + adam_eps)
        )
        free_out[...] = jnp.where(touched, free - update, free)
        moment_out[...] = jnp.where(touched, moment_step, moment)
        second_out[...] = jnp.where(touched, second_step, second)

    return pl.pallas_call(
        kernel,
        out_shape=[f32((label_count, own, units))] + [f32(free_vectors.shape)] * 3,
        compiler_params=params(REST),
        name="down_gradient_and_adam",
    )(coef, ids, every_query, pooled_all, label_grad, free_vectors, moments, seconds)


def body(
    label_count,
    query_count,
    queries,
    label_ids,
    label_text,
    up_weight,
    down_weight,
    free_vectors,
    moments,
    seconds,
):
    label_rows, text_len, model_width = label_text.shape
    query_rows = queries.shape[0]
    unit_cols = up_weight.shape[1]
    labels = label_count * label_rows
    share = label_rows // query_count

    text_rows = label_text.reshape(label_rows * text_len, model_width)
    ids = label_ids.T
    wide_queries = queries.astype(jnp.float32)
    pooled_shares, slope, turned, pooled_text, encoded_part = encode(
        text_rows, up_weight, down_weight, label_rows, label_count
    )
    if query_count == 2:
        encoded = [encoded_part, pair_swap(encoded_part, "query", 2, 1)]
        query_pieces = [queries, pair_swap(wide_queries, "query", 2, 1)]
        id_pieces = [ids, pair_swap(ids, "query", 2, 1)]
    else:
        encoded = [lax.psum(encoded_part, "query")]
        query_pieces = [lax.all_gather(wide_queries, "query", tiled=True)]
        id_pieces = [lax.all_gather(ids, "query", axis=1, tiled=True)]

    own_share, every_query, ids, partial = score(
        encoded, pooled_text, free_vectors, query_pieces, id_pieces, share
    )

    counts = (label_count, query_count)
    tied = lax.optimization_barrier
    score_terms = plane_terms(plane_sum(partial, label_count), label_count)
    vectors = gather_planes(own_share, label_count)
    score_terms, vectors = tied((score_terms, vectors))
    vectors = gather_near(vectors, counts)

    coef, label_grad, keeps, gives = backward(
        score_terms, ids, every_query, down_weight, turned, slope, label_rows, label_count
    )

    gives, vectors = tied((gives, vectors))
    pooled_all = lax.all_to_all(after(pooled_shares, gives), "label", 0, 0)
    given = [gives]
    late = [pooled_all]

    def second_step(gives):
        *gives, late[0] = tied((*gives, late[0]))
        given.append(gives)
        return gives

    def third_step(gives):
        given.append(gives)
        return gives

    def fourth_step(gives):
        given.append(gives)
        return gives

    up_grad = scatter_sum(keeps, gives, label_count, (second_step, third_step, fourth_step))

    vectors = gather_far(after(vectors, given[2]), counts)
    down_cols, free_new, moments_new, seconds_new = down_gradient_and_adam(
        coef,
        ids,
        every_query,
        after(late[0], given[1]).reshape(labels, unit_cols // label_count),
        label_grad,
        free_vectors,
        moments,
        seconds,
        label_count,
    )
    down_rows = lax.all_to_all(after(down_cols, given[1]), "label", 0, 0)
    query_terms = query_gradient(coef, ids, vectors, label_rows)
    down_grad = down_rows.swapaxes(0, 1).reshape(model_width // label_count, unit_cols)
    core = lax.axis_index("query")
    if query_count == 2:
        query_terms = query_terms.reshape(2, query_rows, model_width)
        query_grad = lax.dynamic_index_in_dim(query_terms, core, keepdims=False) + pair_swap(
            lax.dynamic_index_in_dim(query_terms, 1 - core, keepdims=False), "query", 2, 1
        )
    else:
        query_grad = lax.dynamic_slice_in_dim(
            lax.psum(query_terms, "query"), core * query_rows, query_rows
        )
    return (free_new, moments_new, seconds_new, query_grad, up_grad, down_grad)


def solution(mesh):
    placed = (
        P("query", None),
        P("query", None),
        P("label", None, None),
        P(None, "query"),
        P(None, "query"),
        P("label", None),
        P("label", None),
        P("label", None),
    )
    return jax.shard_map(
        functools.partial(body, mesh.shape["label"], mesh.shape["query"]),
        mesh=mesh,
        in_specs=placed,
        out_specs=(
            P("label", None),
            P("label", None),
            P("label", None),
            P("query", None),
            P("label", "query"),
            P("label", "query"),
        ),
        check_vma=False,
    )
```

```python
import functools
import math

import jax
import jax.numpy as jnp
from jax import lax
from jax.experimental import pallas as pl
from jax.experimental.pallas import tpu as pltpu
from jax.sharding import PartitionSpec as P

beta_one = 0.9
beta_two = 0.999
adam_eps = 1e-08
learn_rate = 0.05
first_fix = 1.0 - 0.9**10
second_fix = 1.0 - 0.999**10

PLANE = 4
THIRDS = 3
GELU_ONE = math.sqrt(2.0 / math.pi)
GELU_THREE = GELU_ONE * 0.044715
MIB = 2**20
ENCODE = 28
SCORE = 24
BACKWARD = 32
REST = 24
DOWN = 60
SUMS = 16


def whole(shape):
    return pl.BlockSpec(shape, lambda *_: (0,) * len(shape))


def params(mib):
    return pltpu.CompilerParams(vmem_limit_bytes=mib * MIB)


def f32(shape):
    return jax.ShapeDtypeStruct(shape, jnp.float32)


def bf16(shape):
    return jax.ShapeDtypeStruct(shape, jnp.bfloat16)


def pair_swap(values, axis, count, bits):
    return lax.ppermute(values, axis, [(s, s ^ bits) for s in range(count)])


def parity_swap(values, counts, bits):
    label_count, query_count = counts
    return lax.ppermute(
        values,
        ("label", "query"),
        [
            (s * query_count + q, (s ^ bits[q % 2]) * query_count + q)
            for s in range(label_count)
            for q in range(query_count)
        ],
    )


def plane_sum(values, label_count):
    return values + sum(pair_swap(values, "label", label_count, b) for b in range(1, PLANE))


def plane_terms(values, label_count):
    return [values] + [
        pair_swap(values, "label", label_count, b) for b in range(PLANE, label_count, PLANE)
    ]


def bit_orders(label_count):
    bits = [1 << b for b in range(label_count.bit_length() - 1)]
    return [lead + bits[3:] for lead in ([1, 4, 2], [2, 1, 4], [4, 2, 1])]


def relative_shards(label_count, order):
    count = len(order)
    return [
        sum(bit for place, bit in enumerate(order) if p >> (count - 1 - place) & 1)
        for p in range(label_count)
    ]


def upper(parts):
    size = parts[-1].shape[0]
    return sum(p[size // 2 : size] for p in parts)


def scatter_sum(keeps, gives, label_count, before):
    orders = bit_orders(label_count)

    def swap(values, bit):
        return pair_swap(values, "label", label_count, bit)

    thirds = [[keep, swap(give, order[0])] for keep, give, order in zip(keeps, gives, orders)]
    for step in range(1, 3):
        given = upper_sums(thirds) if step == 1 else [upper(parts) for parts in thirds]
        gives = before[step - 1](given)
        for parts, give, order in zip(thirds, gives, orders):
            parts.append(swap(give, order[step]))
    size = thirds[0][-1].shape[0]
    parts = [jnp.concatenate([sum(p[:size] for p in third) for third in thirds], axis=2)]
    for step in range(3, len(orders[0])):
        give = upper(parts)
        if step == 3:
            (give,) = before[2]([give])
        parts.append(swap(give, orders[0][step]))
    return sum(p[0] for p in parts)


def after(values, *gates):
    return lax.optimization_barrier((values, gates))[0]


def gather_planes(values, label_count):
    return jnp.stack(
        [values]
        + [pair_swap(values, "label", label_count, b) for b in range(PLANE, label_count, PLANE)]
    )


def gather_near(whole_planes, counts):
    return jnp.stack((whole_planes, parity_swap(whole_planes, counts, (1, 2))))


def gather_far(near, counts):
    return jnp.concatenate((near, parity_swap(near, counts, (2, 1))))


def split_bf16(values):
    high = values.astype(jnp.bfloat16)
    low = (values - high.astype(jnp.float32)).astype(jnp.bfloat16)
    return high, low


def gate_of(x):
    square = x * x
    inner = x * (jnp.bfloat16(GELU_ONE) + jnp.bfloat16(GELU_THREE) * square)
    return jnp.bfloat16(0.5) + jnp.bfloat16(0.5) * jnp.tanh(inner), square


def column_steps(cols):
    return 6 if cols % (6 * 128) == 0 else 3


def packs(rows, cols):
    return cols == 96 and rows % 64 == 0


def pack(block):
    rows, cols = block.shape
    if not packs(rows, cols):
        return block
    most, third = rows * 3 // 4, cols // 3
    rest = block[most:]
    beside = [rest[:, p * third : (p + 1) * third] for p in range(3)]
    return jnp.concatenate((block[:most], jnp.concatenate(beside)), axis=1)


def unpack(block, rows, cols):
    if not packs(rows, cols):
        return block
    most = rows * 3 // 4
    few = rows - most
    beside = [block[p * few : (p + 1) * few, cols:] for p in range(3)]
    return jnp.concatenate((block[:, :cols], jnp.concatenate(beside, axis=1)))


def encode(text_rows, up_weight, down_weight, label_rows, label_count):
    tokens, model_width = text_rows.shape
    unit_cols = up_weight.shape[1]
    text_len = tokens // label_rows
    steps = column_steps(unit_cols)
    chunk = unit_cols // steps
    width = model_width // steps
    share = unit_cols // label_count
    packed = (label_rows * 3 // 4, 128) if packs(label_rows, share) else (label_rows, share)

    def pool(values):
        values = values.astype(jnp.float32).reshape(label_rows, text_len, values.shape[1])
        return jnp.sum(values, axis=1) * (1.0 / text_len)

    def kernel(
        text_ref,
        up_ref,
        down_ref,
        shares_ref,
        slope_ref,
        turned_ref,
        mean_ref,
        encoded_ref,
        pooled_ref,
    ):
        step = pl.program_id(0)
        x = jnp.dot(text_ref[...], up_ref[...], preferred_element_type=jnp.float32)
        x = x.astype(jnp.bfloat16)
        gate, square = gate_of(x)
        hidden = x * gate
        inner = jnp.bfloat16(2 * GELU_ONE) + jnp.bfloat16(6 * GELU_THREE) * square
        slope_ref[...] = gate + (hidden - hidden * gate) * inner
        pooled_ref[:, pl.ds(pl.multiple_of(step * chunk, chunk), chunk)] = pool(hidden)
        some = text_ref[:, pl.ds(pl.multiple_of(step * width, width), width)]
        turned_ref[...] = some.T
        mean_ref[...] = pool(some)

        @pl.when(step == steps - 1)
        def _():
            pooled = pooled_ref[...]
            for place in range(label_count):
                shares_ref[place] = pack(pooled[:, place * share : (place + 1) * share])
            both = lax.dot_general(
                jnp.concatenate(split_bf16(pooled)),
                down_ref[...],
                (((1,), (1,)), ((), ())),
                preferred_element_type=jnp.float32,
            )
            encoded_ref[...] = both[:label_rows] + both[label_rows:]

    return pl.pallas_call(
        kernel,
        grid=(steps,),
        in_specs=[
            whole(text_rows.shape),
            pl.BlockSpec((model_width, chunk), lambda i: (0, i)),
            whole(down_weight.shape),
        ],
        out_specs=[
            whole((label_count, *packed)),
            pl.BlockSpec((tokens, chunk), lambda i: (0, i)),
            pl.BlockSpec((width, tokens), lambda i: (i, 0)),
            pl.BlockSpec((label_rows, width), lambda i: (0, i)),
            whole((label_rows, model_width)),
        ],
        out_shape=[
            f32((label_count, *packed)),
            bf16((tokens, unit_cols)),
            bf16((model_width, tokens)),
            f32((label_rows, model_width)),
            f32((label_rows, model_width)),
        ],
        scratch_shapes=[pltpu.VMEM((label_rows, unit_cols), jnp.float32)],
        compiler_params=params(ENCODE),
        name="encode",
    )(text_rows, up_weight, down_weight)


def score(encoded, pooled_text, free_vectors, query_pieces, id_pieces, share):
    label_rows, model_width = free_vectors.shape
    choices = id_pieces[0].shape[0]
    total = sum(p.shape[1] for p in id_pieces)
    terms = len(encoded)
    pieces = len(query_pieces)

    def kernel(*refs):
        encoded_refs, refs = refs[:terms], refs[terms:]
        pooled_ref, free_ref, *refs = refs
        query_refs, refs = refs[:pieces], refs[pieces:]
        id_refs, refs = refs[:pieces], refs[pieces:]
        share_ref, every_ref, ids_ref, partial_ref, label_ref = refs
        core = lax.axis_index("query")
        label_vec = pooled_ref[...] + sum(r[...] for r in encoded_refs) + free_ref[...]
        label_bf = label_vec.astype(jnp.bfloat16)
        label_ref[...] = label_bf.astype(jnp.float32)
        share_ref[...] = label_ref[pl.ds(pl.multiple_of(core * share, share), share), :]
        if pieces == 1:
            every_ref[...] = query_refs[0][...].astype(jnp.bfloat16)
            ids_ref[...] = id_refs[0][...]
        else:
            rows = total // 2
            for place, ref in enumerate(query_refs):
                first = pl.multiple_of((core ^ place) * rows, rows)
                every_ref[pl.ds(first, rows), :] = ref[...].astype(jnp.bfloat16)
            own, other = (r[...] for r in id_refs)
            own_first = core == 0
            ids_ref[...] = jnp.concatenate(
                (jnp.where(own_first, own, other), jnp.where(own_first, other, own)), axis=1
            )
        similar = lax.dot_general(
            label_bf, every_ref[...], (((1,), (1,)), ((), ())), preferred_element_type=jnp.float32
        )
        label = lax.broadcasted_iota(jnp.int32, (label_rows, total), 0)
        label = label + lax.axis_index("label") * label_rows
        for k in range(choices):
            partial_ref[k : k + 1, :] = jnp.sum(
                jnp.where(label == ids_ref[k : k + 1, :], similar, 0.0), axis=0, keepdims=True
            )

    return pl.pallas_call(
        kernel,
        out_shape=[
            f32((share, model_width)),
            bf16((total, model_width)),
            jax.ShapeDtypeStruct((choices, total), jnp.int32),
            f32((choices, total)),
        ],
        scratch_shapes=[pltpu.VMEM((label_rows, model_width), jnp.float32)],
        compiler_params=params(SCORE),
        name="score",
    )(*encoded, pooled_text, free_vectors, *query_pieces, *id_pieces)


def spread_of(ids_ref, coef, first, labels):
    choices, total = coef.shape
    label = lax.broadcasted_iota(jnp.int32, (labels, total), 0) + first
    spread = jnp.zeros((labels, total), jnp.float32)
    for k in range(choices):
        spread = jnp.where(label == ids_ref[k : k + 1, :], coef[k : k + 1, :], spread)
    return spread.astype(jnp.bfloat16)


def backward(score_terms, ids, every_query, down_weight, turned, slope, label_rows, label_count):
    choices, total = ids.shape
    model_width, unit_cols = down_weight.shape
    tokens = turned.shape[1]
    text_len = tokens // label_rows
    cols = unit_cols // THIRDS
    own = model_width // label_count
    half = label_count // 2
    terms = len(score_terms)
    temper = 1.0 / math.sqrt(model_width)
    relative = [relative_shards(label_count, order) for order in bit_orders(label_count)]

    def kernel(*refs):
        score_refs, refs = refs[:terms], refs[terms:]
        shard = lax.axis_index("label")
        ids_ref, query_ref, down_ref, *refs = refs
        turned_ref, slope_ref, coef_ref, grad_ref, *refs = refs
        outs, refs = refs[: 2 * THIRDS], refs[2 * THIRDS :]
        blocks_ref, kept_ref, given_ref, out_sem = refs

        scores = sum(r[...] for r in score_refs) * temper
        powers = jnp.exp(scores - jnp.max(scores, axis=0, keepdims=True))
        likely = powers / jnp.sum(powers, axis=0, keepdims=True)
        rank = lax.broadcasted_iota(jnp.int32, (choices, total), 0)
        coef = (likely - jnp.where(rank < 2, 0.5, 0.0)) * temper
        coef = coef.astype(jnp.bfloat16).astype(jnp.float32)
        coef_ref[...] = coef
        spread = spread_of(ids_ref, coef, shard * label_rows, label_rows)
        grad = jnp.dot(spread, query_ref[...], preferred_element_type=jnp.float32)
        grad_ref[...] = grad
        out_grad = grad.astype(jnp.bfloat16)

        flights = []
        for third in range(THIRDS):
            span = slice(third * cols, (third + 1) * cols)
            hidden_grad = jnp.dot(
                out_grad, down_ref[:, span], preferred_element_type=jnp.float32
            ) * (1.0 / text_len)
            preact_grad = (
                slope_ref[:, span].astype(jnp.float32).reshape(label_rows, text_len, cols)
                * hidden_grad[:, None, :]
            )
            up_term = jnp.dot(
                turned_ref[...],
                preact_grad.reshape(tokens, cols).astype(jnp.bfloat16),
                preferred_element_type=jnp.float32,
            )
            for block in range(label_count):
                blocks_ref[block] = up_term[block * own : (block + 1) * own, :]
            for p in range(half):
                given_ref[third, p] = blocks_ref[shard ^ relative[third][half + p]]
                kept_ref[third, p] = blocks_ref[shard ^ relative[third][p]]
            for side, buffer in enumerate((kept_ref, given_ref)):
                place = 2 * third + side
                flight = pltpu.make_async_copy(buffer.at[third], outs[place], out_sem.at[place])
                flight.start()
                flights.append(flight)
        for flight in flights:
            flight.wait()

    outs = pl.pallas_call(
        kernel,
        in_specs=[pl.BlockSpec(memory_space=pltpu.VMEM)] * (terms + 5),
        out_specs=[pl.BlockSpec(memory_space=pltpu.VMEM)] * 2
        + [pl.BlockSpec(memory_space=pl.ANY)] * (2 * THIRDS),
        out_shape=[f32((choices, total)), f32((label_rows, model_width))]
        + [f32((half, own, cols))] * (2 * THIRDS),
        scratch_shapes=[pltpu.VMEM((label_count, own, cols), jnp.float32)]
        + [pltpu.VMEM((THIRDS, half, own, cols), jnp.float32)] * 2
        + [pltpu.SemaphoreType.DMA((2 * THIRDS,))],
        compiler_params=params(BACKWARD),
        cost_estimate=pl.CostEstimate(
            flops=2 * tokens * model_width * unit_cols,
            bytes_accessed=16 * MIB,
            transcendentals=choices * total,
        ),
        name="backward",
    )(*score_terms, ids, every_query, down_weight, turned, slope)
    return outs[0], outs[1], outs[2::2], outs[3::2]


def query_gradient(coef, ids, vectors, label_rows):
    choices, total = ids.shape
    near, planes, share, model_width = vectors.shape
    rows = near * planes * share

    def kernel(coef_ref, ids_ref, vector_ref, out_ref):
        core = lax.axis_index("query")
        row = lax.broadcasted_iota(jnp.int32, (rows, total), 0)
        block = row // share
        plane, place = block % planes, block // planes
        turned = place // 2 + place % 2 * 2
        place = jnp.where(lax.rem(core, 2) == 0, place, turned)
        owner = lax.axis_index("label") ^ (plane * PLANE + place)
        label = owner * label_rows + core * share + row % share
        spread = jnp.zeros((rows, total), jnp.float32)
        for k in range(choices):
            spread = jnp.where(label == ids_ref[k : k + 1, :], coef_ref[k : k + 1, :], spread)
        out_ref[...] = lax.dot_general(
            spread.astype(jnp.bfloat16),
            vector_ref[...].reshape(rows, model_width).astype(jnp.bfloat16),
            (((0,), (0,)), ((), ())),
            preferred_element_type=jnp.float32,
        )

    return pl.pallas_call(
        kernel,
        out_shape=f32((total, model_width)),
        compiler_params=params(REST),
        name="query_gradient",
    )(coef, ids, vectors)


def down_gradient(coef, ids, every_query, pooled_all, label_count, units, label_rows):
    model_width = every_query.shape[1]
    own = model_width // label_count

    def product(left, right):
        both = lax.dot_general(
            left,
            jnp.concatenate(split_bf16(right), axis=1),
            (((0,), (0,)), ((), ())),
            preferred_element_type=jnp.float32,
        )
        return both[:, :units] + both[:, units:]

    def kernel(coef_ref, ids_ref, query_ref, pooled_ref, out_ref):
        spread = spread_of(ids_ref, coef_ref[...], 0, label_count * label_rows)
        pooled = jnp.concatenate(
            [unpack(pooled_ref[place], label_rows, units) for place in range(label_count)]
        )
        result = product(query_ref[...], product(spread, pooled))
        for block in range(label_count):
            out_ref[block] = result[block * own : (block + 1) * own, :]

    return pl.pallas_call(
        kernel,
        out_shape=f32((label_count, own, units)),
        compiler_params=params(DOWN),
        name="down_gradient",
    )(coef, ids, every_query, pooled_all)


def adam(ids, label_grad, free_vectors, moments, seconds):
    choices, total = ids.shape
    label_rows = free_vectors.shape[0]

    def kernel(ids_ref, grad_ref, free_ref, moment_ref, second_ref, *outs):
        free_out, moment_out, second_out = outs
        label = lax.broadcasted_iota(jnp.int32, (label_rows, total), 0)
        label = label + lax.axis_index("label") * label_rows
        hits = jnp.zeros((label_rows, total), jnp.float32)
        for k in range(choices):
            hits = jnp.where(label == ids_ref[k : k + 1, :], 1.0, hits)
        touched = jnp.max(hits, axis=1, keepdims=True) > 0.5
        grad, free, moment, second = (r[...] for r in (grad_ref, free_ref, moment_ref, second_ref))
        moment_step = beta_one * moment + (1.0 - beta_one) * grad
        second_step = beta_two * second + (1.0 - beta_two) * grad * grad
        update = (
            learn_rate
            * (moment_step / first_fix)
            / (jnp.sqrt(second_step / second_fix) + adam_eps)
        )
        free_out[...] = jnp.where(touched, free - update, free)
        moment_out[...] = jnp.where(touched, moment_step, moment)
        second_out[...] = jnp.where(touched, second_step, second)

    return pl.pallas_call(
        kernel,
        out_shape=[f32(free_vectors.shape)] * 3,
        compiler_params=params(REST),
        name="adam",
    )(ids, label_grad, free_vectors, moments, seconds)


def upper_sums(held):
    size, own, cols = held[0][-1].shape
    half = size // 2
    steps = 2 if half % 2 == 0 else 1
    block = half // steps
    count = len(held[0])

    def kernel(*refs):
        ins, outs = refs[: THIRDS * count], refs[THIRDS * count :]
        for third, out in enumerate(outs):
            out[...] = sum(r[...] for r in ins[third * count : (third + 1) * count])

    return pl.pallas_call(
        kernel,
        grid=(steps,),
        in_specs=[pl.BlockSpec((block, own, cols), lambda i: (steps + i, 0, 0))] * (THIRDS * count),
        out_specs=[pl.BlockSpec((block, own, cols), lambda i: (i, 0, 0))] * THIRDS,
        out_shape=[f32((half, own, cols))] * THIRDS,
        compiler_params=params(SUMS),
        name="upper_sums",
    )(*[part for parts in held for part in parts])


def joined_sums(held):
    size, own, cols = held[0][-1].shape
    half = size // 2
    count = len(held[0])

    def kernel(*refs):
        ins, (keep_ref, give_ref) = refs[:-2], refs[-2:]
        for third in range(THIRDS):
            span = slice(third * cols, (third + 1) * cols)
            some = ins[third * count : (third + 1) * count]
            keep_ref[:, :, span] = sum(r[:half] for r in some)
            give_ref[:, :, span] = sum(r[half:] for r in some)

    return pl.pallas_call(
        kernel,
        grid=(1,),
        in_specs=[pl.BlockSpec((size, own, cols), lambda i: (0, 0, 0))] * (THIRDS * count),
        out_specs=[whole((half, own, THIRDS * cols))] * 2,
        out_shape=[f32((half, own, THIRDS * cols))] * 2,
        compiler_params=params(SUMS),
        name="joined_sums",
    )(*[part for parts in held for part in parts])


def body(
    label_count,
    query_count,
    queries,
    label_ids,
    label_text,
    up_weight,
    down_weight,
    free_vectors,
    moments,
    seconds,
):
    label_rows, text_len, model_width = label_text.shape
    query_rows = queries.shape[0]
    unit_cols = up_weight.shape[1]
    labels = label_count * label_rows
    share = label_rows // query_count

    text_rows = label_text.reshape(label_rows * text_len, model_width)
    ids = label_ids.T
    wide_queries = queries.astype(jnp.float32)
    pooled_shares, slope, turned, pooled_text, encoded_part = encode(
        text_rows, up_weight, down_weight, label_rows, label_count
    )
    if query_count == 2:
        encoded = [encoded_part, pair_swap(encoded_part, "query", 2, 1)]
        query_pieces = [queries, pair_swap(wide_queries, "query", 2, 1)]
        id_pieces = [ids, pair_swap(ids, "query", 2, 1)]
    else:
        encoded = [lax.psum(encoded_part, "query")]
        query_pieces = [lax.all_gather(wide_queries, "query", tiled=True)]
        id_pieces = [lax.all_gather(ids, "query", axis=1, tiled=True)]

    own_share, every_query, ids, partial = score(
        encoded, pooled_text, free_vectors, query_pieces, id_pieces, share
    )

    counts = (label_count, query_count)
    tied = lax.optimization_barrier
    score_terms = plane_terms(plane_sum(partial, label_count), label_count)
    vectors = gather_planes(own_share, label_count)
    score_terms, vectors = tied((score_terms, vectors))
    vectors = gather_near(vectors, counts)

    coef, label_grad, keeps, gives = backward(
        score_terms, ids, every_query, down_weight, turned, slope, label_rows, label_count
    )

    gives, vectors = tied((gives, vectors))
    pooled_all = lax.all_to_all(after(pooled_shares, gives), "label", 0, 0)
    given = [gives]
    late = [pooled_all]

    def second_step(gives):
        *gives, late[0] = tied((*gives, late[0]))
        given.append(gives)
        return gives

    def third_step(gives):
        given.append(gives)
        return gives

    def fourth_step(gives):
        given.append(gives)
        return gives

    up_grad = scatter_sum(keeps, gives, label_count, (second_step, third_step, fourth_step))

    vectors = gather_far(after(vectors, given[2]), counts)
    down_cols = down_gradient(
        coef,
        ids,
        every_query,
        after(late[0], given[1]),
        label_count,
        unit_cols // label_count,
        label_rows,
    )
    free_new, moments_new, seconds_new = adam(
        ids, after(label_grad, given[3]), free_vectors, moments, seconds
    )
    down_rows = lax.all_to_all(after(down_cols, given[1]), "label", 0, 0)
    query_terms = query_gradient(coef, ids, vectors, label_rows)
    down_grad = down_rows.swapaxes(0, 1).reshape(model_width // label_count, unit_cols)
    core = lax.axis_index("query")
    if query_count == 2:
        query_terms = query_terms.reshape(2, query_rows, model_width)
        query_grad = lax.dynamic_index_in_dim(query_terms, core, keepdims=False) + pair_swap(
            lax.dynamic_index_in_dim(query_terms, 1 - core, keepdims=False), "query", 2, 1
        )
    else:
        query_grad = lax.dynamic_slice_in_dim(
            lax.psum(query_terms, "query"), core * query_rows, query_rows
        )
    return (free_new, moments_new, seconds_new, query_grad, up_grad, down_grad)


def solution(mesh):
    placed = (
        P("query", None),
        P("query", None),
        P("label", None, None),
        P(None, "query"),
        P(None, "query"),
        P("label", None),
        P("label", None),
        P("label", None),
    )
    return jax.shard_map(
        functools.partial(body, mesh.shape["label"], mesh.shape["query"]),
        mesh=mesh,
        in_specs=placed,
        out_specs=(
            P("label", None),
            P("label", None),
            P("label", None),
            P("query", None),
            P("label", "query"),
            P("label", "query"),
        ),
        check_vma=False,
    )
```
